32 devices in a mesh: gx: 4 (over y, core), gy: 8 (over z, x).
Axes of the slice: x: 2, y: 2, z: 4, core: 2. Of those that a mesh axis runs over, the one named last changes fastest.
Arguments:
- right_side: float32 [4, 8, 176, 1152], P('gx', 'gy'), may hold values from -6 to 6
- flex: bfloat16 [4, 8, 1152, 1152], P('gx', 'gy'), as said below
- stiff: bfloat16 [4, 8, 1152, 1152], P('gx', 'gy')
- coarse_inv: float32 [3072, 3072], P('gx', 'gy'), as said below
- corner_map: int32 [4, 8, 24], P('gx', 'gy'), may hold values from 0 to 3071
- side_rows: int32 [4, 8, 2], P('gx', 'gy'), may hold values from 1 to 288, as said below
Outputs:
- solution: float32 [4, 8, 176, 1152], P('gx', 'gy')
- residual: float32 [4, 8, 176, 1152], P('gx', 'gy')
- resid_norm: float32 [3, 176], replicated
The draws below stay inside these ranges and needn't reach their ends.
Inputs may be any that keep to these rules, and one draw needn't show every extreme that they name: Entry 0 of side_rows at the first subdomain equals 288. flex and stiff are near one on the diagonal plus small full off-diagonal parts. coarse_inv is a dense matrix.
All inputs are finite; a program needn't handle non-finite values.
Results may differ from the reference program's by a relative error of at most 0.0056.
Values sent between devices are 32-bit elements; how exact they have to be, the bound alone decides.
A program may use at most 64 MiB of HBM per device.

```python
import jax
import jax.numpy as jnp
from jax import lax

M = 1152
SIDE = 288
COARSE = 3072
CORN = 24
LOADS = 176
ITERS = 3
N_GX = 4
N_GY = 8


def dominant_block(key, count, order, spread):
    noise = jax.random.normal(key, (count, order, order), jnp.float32)
    return jnp.eye(order, dtype=jnp.float32)[None] + noise * (spread / order ** 0.5)


def draw_flex(key, part):
    blocks = dominant_block(jax.random.fold_in(key, 11), N_GX * N_GY, M, 0.3)
    return blocks.reshape((N_GX, N_GY, M, M)).astype(jnp.bfloat16)


def draw_stiff(key, part):
    blocks = dominant_block(jax.random.fold_in(key, 23), N_GX * N_GY, M, 0.3)
    return blocks.reshape((N_GX, N_GY, M, M)).astype(jnp.bfloat16)


def draw_coarse_inv(key, part):
    blocks = dominant_block(jax.random.fold_in(key, 37), 1, COARSE, 0.3)
    return (blocks[0] * 0.6).astype(jnp.float32)


def draw_side_rows(key, part):
    counts = jax.random.randint(jax.random.fold_in(key, 41), (N_GX, N_GY, 2), 1, SIDE + 1)
    return counts.at[0, 0, 0].set(SIDE).astype(jnp.int32)


def touch_ends(drawn, rng, least, largest):
    index_at = [jax.random.randint(jax.random.fold_in(rng, axis), (), 0, length) for axis, length in enumerate(drawn.shape)]
    main_axis = drawn.shape.index(max(drawn.shape))
    neighbour = index_at[:main_axis] + [(index_at[main_axis] + 1) % drawn.shape[main_axis]] + index_at[main_axis + 1:]
    return drawn.at[tuple(index_at)].set(least).at[tuple(neighbour)].set(largest)


def level_of(stream_key, shape, pieces, low, high):
    gain = 1.0
    for dim, shards_of in pieces:
        steps = jax.random.uniform(jax.random.fold_in(jax.random.fold_in(stream_key, 6), dim), (shards_of,), jnp.float32, low / len(pieces), high / len(pieces))
        gain = gain * jnp.repeat(jnp.exp(steps), shape[dim] // shards_of).reshape((-1,) + (1,) * (len(shape) - 1 - dim))
    return gain


def normal_values(rng, dims, width, bound, cuts=(), held_as=jnp.bfloat16):
    values = width * jax.random.normal(rng, dims, jnp.float32)
    if cuts:
        values = values * level_of(rng, dims, cuts, -0.22, 0.18)
    return jnp.clip(values, -bound, bound).astype(held_as)


def setup_inputs(seed: int = 0) -> dict:
    keys = jax.random.split(jax.random.key(seed), 7)
    return {
        "right_side": normal_values(keys[0], (N_GX, N_GY, LOADS, M), 1.0, 6.0, ((0, 4), (1, 8)), jnp.float32),
        "flex": draw_flex(jax.random.fold_in(keys[6], 71), 0),
        "stiff": draw_stiff(jax.random.fold_in(keys[6], 71), 0),
        "coarse_inv": draw_coarse_inv(jax.random.fold_in(keys[6], 71), 0),
        "corner_map": touch_ends(jax.random.randint(keys[4], (N_GX, N_GY, CORN), 0, COARSE), jax.random.fold_in(keys[4], 1), 0, COARSE - 1).astype(jnp.int32),
        "side_rows": draw_side_rows(jax.random.fold_in(keys[6], 71), 0),
    }


cheb_center = 1.15
cheb_half = 0.85
cheb_sigma = cheb_center / cheb_half

def local_product(vectors, blocks):

    def single(pair):
        return lax.dot_general(pair[0], pair[1], (((1,), (1,)), ((), ())), preferred_element_type=jnp.float32)
    shape = vectors.shape
    flat_vec = vectors.reshape((-1,) + shape[2:])
    flat_blk = blocks.reshape((-1,) + blocks.shape[2:])
    return lax.map(single, (flat_vec, flat_blk)).reshape(shape[:3] + (blocks.shape[2],))

def apply_operator(field, flex, stiff, coarse_inv, corner_map, side_rows):
    flexed = local_product(field.astype(jnp.bfloat16), flex)
    side = flexed.shape[-1] // 4
    west_side = flexed[..., 0:side]
    east_side = flexed[..., side:2 * side]
    north_side = flexed[..., 2 * side:3 * side]
    south_side = flexed[..., 3 * side:4 * side]
    row_ids = jnp.arange(side)
    grid_cols = jnp.arange(N_GY)
    grid_rows = jnp.arange(N_GX)
    mask_east = ((row_ids[None, None, :] < side_rows[:, :, 0:1]) & (grid_cols[None, :, None] < N_GY - 1)).astype(jnp.float32)
    mask_south = ((row_ids[None, None, :] < side_rows[:, :, 1:2]) & (grid_rows[:, None, None] < N_GX - 1)).astype(jnp.float32)
    from_east = jnp.concatenate([west_side[:, 1:], jnp.zeros_like(west_side[:, :1])], axis=1)
    jump_east = mask_east[:, :, None, :] * (east_side - from_east)
    back_west = jnp.concatenate([jnp.zeros_like(jump_east[:, :1]), jump_east[:, :-1]], axis=1)
    from_south = jnp.concatenate([north_side[1:], jnp.zeros_like(north_side[:1])], axis=0)
    jump_south = mask_south[:, :, None, :] * (south_side - from_south)
    back_north = jnp.concatenate([jnp.zeros_like(jump_south[:1]), jump_south[:-1]], axis=0)
    balanced = jnp.concatenate([west_side + 0.5 * back_west, east_side - 0.5 * jump_east, north_side + 0.5 * back_north, south_side - 0.5 * jump_south], axis=-1)
    stiffed = local_product(balanced.astype(jnp.bfloat16), stiff)
    corners = corner_map.shape[-1]
    corner_vals = stiffed[..., :corners]
    flat_vals = jnp.transpose(corner_vals, (0, 1, 3, 2)).reshape((-1, corner_vals.shape[2]))
    coarse_rhs = jax.ops.segment_sum(flat_vals, corner_map.reshape(-1), num_segments=coarse_inv.shape[0])
    coarse_sol = jnp.dot(coarse_inv, coarse_rhs, precision=lax.Precision.HIGHEST)
    correction = jnp.transpose(coarse_sol[corner_map], (0, 1, 3, 2))
    return jnp.concatenate([corner_vals + correction, stiffed[..., corners:]], axis=-1)

def reference(right_side, flex, stiff, coarse_inv, corner_map, side_rows):
    solution = jnp.zeros_like(right_side)
    residual = right_side
    direction = residual / cheb_center
    rho_prev = 1.0 / cheb_sigma
    norm_list = []
    for iteration in range(ITERS):
        solution = solution + direction
        residual = residual - apply_operator(direction, flex, stiff, coarse_inv, corner_map, side_rows)
        norm_list.append(jnp.sqrt(lax.optimization_barrier(jnp.sum(residual * residual, axis=(0, 1, 3))) / (N_GX * N_GY * M)))
        if iteration + 1 < ITERS:
            rho_next = 1.0 / (2.0 * cheb_sigma - rho_prev)
            direction = rho_next * rho_prev * direction + 2.0 * rho_next / cheb_half * residual
            rho_prev = rho_next
    return (solution, residual, jnp.stack(norm_list))
```

```python
import functools

import jax
import jax.numpy as jnp
from jax import lax
from jax.experimental import pallas as pl
from jax.experimental.pallas import tpu as pltpu
from jax.sharding import PartitionSpec as P

ITERS = 3

cheb_center = 1.15
cheb_half = 0.85
cheb_sigma = cheb_center / cheb_half

MESH = pl.DeviceIdType.MESH
OPP = (1, 0, 3, 2)


def remote(src, dst, send_sem, recv_sem, device):
    return pltpu.make_async_remote_copy(
        src_ref=src,
        dst_ref=dst,
        send_sem=send_sem,
        recv_sem=recv_sem,
        device_id=device,
        device_id_type=MESH,
    )


def kernel(
    n_gx, n_gy, corners,
    rhs_ref, flex_ref, stiff_hbm, cinv_hbm, info_ref,
    sol_ref, res_ref, norm_ref,
    stiff_ref, cinv_ref, cbf_ref, info_all, ids_ref, part_ref, from_core, from_y, own_rows, from_gy, coarse_ref,
    dir_ref, dbf_ref, bal_ref, flexed_ref, recv_ref, vals_ref, norm_gy, norm_gx,
    local_sem, side_send, side_recv, gat_send, gat_recv, set_send, set_recv, nrm_send, nrm_recv,
):
    row = lax.axis_index("gx")
    col = lax.axis_index("gy")
    core = lax.rem(row, 2)
    chip = lax.div(row, 2)
    n_y = n_gx // 2
    order, loads = rhs_ref.shape
    side = order // 4
    n_sub = n_gx * n_gy
    rows_c, cols_c = cinv_ref.shape
    sibling = (chip * 2 + 1 - core, col)
    pending = []

    copy_stiff = pltpu.make_async_copy(stiff_hbm, stiff_ref, local_sem.at[0])
    copy_cinv = pltpu.make_async_copy(cinv_hbm, cinv_ref, local_sem.at[1])
    copy_stiff.start()
    copy_cinv.start()

    barrier = pltpu.get_barrier_semaphore()
    gy_peers = [(row, lax.rem(col + k, n_gy)) for k in range(1, n_gy)]
    gx_peers = [(lax.rem(row + k, n_gx), col) for k in range(1, n_gx)]
    for peer in gy_peers + gx_peers:
        pl.semaphore_signal(barrier, inc=1, device_id=peer, device_id_type=MESH)

    has = (col > 0, col < n_gy - 1, row > 0, row < n_gx - 1)
    neighbour = (
        (row, jnp.maximum(col - 1, 0)),
        (row, jnp.minimum(col + 1, n_gy - 1)),
        (jnp.maximum(row - 1, 0), col),
        (jnp.minimum(row + 1, n_gx - 1), col),
    )
    info_all[row, pl.ds(pl.multiple_of(col * 8, 8), 8)] = info_ref[...]
    direction = rhs_ref[...] * (1.0 / cheb_center)
    dir_ref[...] = direction
    dbf_ref[...] = direction.astype(jnp.bfloat16)
    for s in range(4):
        @pl.when(jnp.logical_not(has[s]))
        def _():
            for it in range(ITERS):
                recv_ref[it, s] = jnp.zeros((side, loads), jnp.float32)

    pl.semaphore_wait(barrier, n_gy - 1 + n_gx - 1)

    def gather_start(buf, height, g):
        mine = buf.at[row, pl.ds(pl.multiple_of(col * height, 8), height)]
        copies = []
        for k in range(1, n_gy):
            c = remote(mine, mine, gat_send.at[g, k], gat_recv.at[g, k], gy_peers[k - 1])
            c.start()
            copies.append(c)
        pending.extend(copies)
        return copies

    def gather_finish(buf, g, copies):
        for c in copies:
            c.wait_recv()
        base = n_gy
        slab = buf.at[row]
        across = []
        for j in range(1, n_y):
            peer = (lax.rem(chip + j, n_y) * 2 + core, col)
            c = remote(slab, slab, gat_send.at[g, base + j], gat_recv.at[g, base + j], peer)
            c.start()
            across.append(c)
        base = n_gy + n_y
        c = remote(slab, slab, gat_send.at[g, base], gat_recv.at[g, base], sibling)
        c.start()
        twin = [c]
        for j in range(1, n_y):
            across[j - 1].wait_recv()
            arrived = buf.at[lax.rem(chip + n_y - j, n_y) * 2 + core]
            c = remote(arrived, arrived, gat_send.at[g, base + j], gat_recv.at[g, base + j], sibling)
            c.start()
            twin.append(c)
        for c in twin:
            c.wait_recv()
        pending.extend(across + twin)

    def side_copy(it, s):
        return remote(
            flexed_ref.at[it, s], recv_ref.at[it, OPP[s]], side_send.at[it, s], side_recv.at[it, OPP[s]], neighbour[s]
        )

    def side_arrival(it, s):
        return remote(
            flexed_ref.at[it, s], recv_ref.at[it, s], side_send.at[it, s], side_recv.at[it, s], neighbour[s]
        )

    info_copies = gather_start(info_all, 8, ITERS)

    for s in range(4):
        flexed_ref[0, s] = jnp.dot(
            flex_ref[s * side : (s + 1) * side, :], dbf_ref[...], preferred_element_type=jnp.float32
        )

        @pl.when(has[s])
        def _():
            side_copy(0, s).start()

    copy_cinv.wait()
    if cbf_ref.shape[1] > cols_c:
        cbf_ref[...] = jnp.zeros(cbf_ref.shape, jnp.bfloat16)
    cbf_ref[:, 0:cols_c] = cinv_ref[...].astype(jnp.bfloat16)
    gather_finish(info_all, ITERS, info_copies)

    lane = lax.broadcasted_iota(jnp.int32, (corners, 128), 1)
    sub = lax.broadcasted_iota(jnp.int32, (corners, 128), 0)
    for a in range(n_gx):
        for b in range(n_gy):
            line = jnp.broadcast_to(info_all[a, b * 8 : b * 8 + 1, :], (corners, 128))
            column = jnp.sum(jnp.where(lane == sub, line, 0.0), axis=1, keepdims=True)
            ids_ref[a, b * corners : (b + 1) * corners, :] = jnp.broadcast_to(column, (corners, 128))

    strip = n_gy * corners
    row_iota = lax.broadcasted_iota(jnp.int32, (strip, rows_c), 1).astype(jnp.float32)
    row_base = (row * rows_c).astype(jnp.float32)
    for a in range(n_gx):
        pick = jnp.where(ids_ref[a][:, 0:1] - row_base == row_iota, 1.0, 0.0).astype(jnp.bfloat16)
        part_ref[a] = jnp.dot(pick, cbf_ref[...], preferred_element_type=jnp.float32)
    to_core = []
    for j in range(n_y):
        c = remote(
            part_ref.at[2 * j + 1 - core], from_core.at[j], set_send.at[j], set_recv.at[j], sibling
        )
        c.start()
        to_core.append(c)
    pending.extend(to_core)

    def lines_at(a, b, entry):
        base = pl.multiple_of(b * 8, 8)
        return info_all[a, pl.ds(base, 8), :][1:2, entry : entry + 1]

    west_of = lax.rem(col + n_gy - 1, n_gy)
    north_of = lax.rem(row + n_gx - 1, n_gx)
    limits = (
        lines_at(row, west_of, 0) * jnp.where(has[0], 1.0, 0.0),
        lines_at(row, col, 0) * jnp.where(has[1], 1.0, 0.0),
        lines_at(north_of, col, 1) * jnp.where(has[2], 1.0, 0.0),
        lines_at(row, col, 1) * jnp.where(has[3], 1.0, 0.0),
    )
    side_iota = lax.broadcasted_iota(jnp.int32, (side, loads), 0).astype(jnp.float32)

    for c in to_core:
        c.wait_recv()
    to_y = []
    for j in range(1, n_y):
        target = lax.rem(chip + j, n_y)
        from_core[target] = from_core[target] + part_ref[2 * target + core]
        c = remote(
            from_core.at[target], from_y.at[j - 1], set_send.at[n_y + j - 1], set_recv.at[n_y + j - 1],
            (target * 2 + core, col),
        )
        c.start()
        to_y.append(c)
    pending.extend(to_y)

    copy_stiff.wait()

    rho_prev = 1.0 / cheb_sigma
    for it in range(ITERS):
        sol_ref[...] = dir_ref[...] if it == 0 else sol_ref[...] + dir_ref[...]
        for s in (2, 3, 0, 1):
            @pl.when(has[s])
            def _():
                side_arrival(it, s).wait_recv()

            own = flexed_ref[it, s]
            jump = jnp.where(side_iota < limits[s], recv_ref[it, s] - own, 0.0)
            bal_ref[s * side : (s + 1) * side, :] = (own + 0.5 * jump).astype(jnp.bfloat16)

        head = jnp.dot(stiff_ref[0:32, :], bal_ref[...], preferred_element_type=jnp.float32)
        corner_vals = head[0:corners]
        vals_ref[it, row, pl.ds(pl.multiple_of(col * corners, 8), corners)] = corner_vals
        val_copies = gather_start(vals_ref.at[it], corners, it)

        rest = jnp.dot(stiff_ref[32:, :], bal_ref[...], preferred_element_type=jnp.float32)
        before = rhs_ref if it == 0 else res_ref
        mid = before[corners:32] - head[corners:]
        low = before[32:] - rest
        res_ref[corners:32] = mid
        res_ref[32:] = low
        squares = jnp.sum(low * low, axis=0, keepdims=True) + jnp.sum(mid * mid, axis=0, keepdims=True)
        last = it + 1 == ITERS
        if not last:
            rho_next = 1.0 / (2.0 * cheb_sigma - rho_prev)
            keep, gain = rho_next * rho_prev, 2.0 * rho_next / cheb_half
            rho_prev = rho_next
            later = keep * dir_ref[corners:] + gain * res_ref[corners:]
            dir_ref[corners:] = later
            dbf_ref[128:, :] = later[128 - corners :].astype(jnp.bfloat16)
            for s in range(4):
                flexed_ref[it + 1, s] = jnp.dot(
                    flex_ref[s * side : (s + 1) * side, 128:], dbf_ref[128:, :], preferred_element_type=jnp.float32
                )

        if it == 0:
            own_strip = from_core[chip] + part_ref[2 * chip + core]
            for j in range(1, n_y):
                to_y[j - 1].wait_recv()
                own_strip = own_strip + from_y[j - 1]
            for b in range(n_gy):
                own_rows[b] = own_strip[b * corners : (b + 1) * corners]
            base = 2 * n_y
            from_gy[col] = own_rows[col]
            to_gy = []
            for k in range(1, n_gy):
                c = remote(
                    own_rows.at[lax.rem(col + k, n_gy)], from_gy.at[col],
                    set_send.at[base + k], set_recv.at[base + k], gy_peers[k - 1],
                )
                c.start()
                to_gy.append(c)
            pending.extend(to_gy)

        gather_finish(vals_ref.at[it], it, val_copies)

        if it == 0:
            for c in to_gy:
                c.wait_recv()
            col_iota = lax.broadcasted_iota(jnp.int32, (strip, cbf_ref.shape[1]), 1).astype(jnp.float32)
            strips = []
            for a in range(n_gx):
                def add(b, total):
                    base_col = (b * cols_c).astype(jnp.float32)
                    pick = jnp.where(ids_ref[a][:, 0:1] - base_col == col_iota, 1.0, 0.0).astype(jnp.bfloat16)
                    return total + lax.dot_general(
                        from_gy[b].astype(jnp.bfloat16), pick, (((1,), (1,)), ((), ())),
                        preferred_element_type=jnp.float32,
                    )

                strips.append(lax.fori_loop(0, n_gy, add, jnp.zeros((corners, strip), jnp.float32)))
            coarse_ref[...] = jnp.concatenate(strips, axis=1)

        fixed = corner_vals + jnp.dot(
            coarse_ref[...].astype(jnp.bfloat16),
            vals_ref[it].reshape(n_sub * corners, loads).astype(jnp.bfloat16),
            preferred_element_type=jnp.float32,
        )
        top = before[0:corners] - fixed
        res_ref[0:corners] = top
        squares = squares + jnp.sum(top * top, axis=0, keepdims=True)
        norm_gy[col, it : it + 1, :] = squares
        if not last:
            dir_ref[0:corners] = keep * dir_ref[0:corners] + gain * top
            dbf_ref[0:128, :] = dir_ref[0:128].astype(jnp.bfloat16)
            for s in range(4):
                flexed_ref[it + 1, s] += jnp.dot(
                    flex_ref[s * side : (s + 1) * side, 0:128], dbf_ref[0:128, :], preferred_element_type=jnp.float32
                )

                @pl.when(has[s])
                def _():
                    side_copy(it + 1, s).start()

    mine = norm_gy.at[col]
    sums = []
    for k in range(1, n_gy):
        c = remote(mine, mine, nrm_send.at[k], nrm_recv.at[k], gy_peers[k - 1])
        c.start()
        sums.append(c)
    for c in sums:
        c.wait_recv()
    total = norm_gy[0, 0:ITERS]
    for b in range(1, n_gy):
        total = total + norm_gy[b, 0:ITERS]
    norm_gx[row, 0:ITERS] = total
    mine = norm_gx.at[row]
    wide = []
    for k in range(1, n_gx):
        c = remote(mine, mine, nrm_send.at[n_gy + k], nrm_recv.at[n_gy + k], gx_peers[k - 1])
        c.start()
        wide.append(c)
    for c in wide:
        c.wait_recv()
    total = norm_gx[0, 0:ITERS]
    for a in range(1, n_gx):
        total = total + norm_gx[a, 0:ITERS]
    norm_ref[...] = jnp.sqrt(total / (n_sub * order))

    for c in pending + sums + wide:
        c.wait_send()
    for s in range(4):
        @pl.when(has[s])
        def _():
            for it in range(ITERS):
                side_copy(it, s).wait_send()


def local(right_side, flex, stiff, coarse_inv, corner_map, side_rows):
    n_gx = lax.axis_size("gx")
    n_gy = lax.axis_size("gy")
    n_y = n_gx // 2
    loads, order = right_side.shape[2:]
    corners = corner_map.shape[2]
    side = order // 4
    rows_c, cols_c = coarse_inv.shape
    strip = n_gy * corners
    cols_p = -(-cols_c // 128) * 128
    info = jnp.concatenate(
        [
            jnp.pad(corner_map[0].astype(jnp.float32), ((0, 0), (0, 128 - corners))),
            jnp.pad(side_rows[0].astype(jnp.float32), ((0, 6), (0, 126))),
        ]
    )
    f32, bf16 = jnp.float32, jnp.bfloat16
    vmem = pl.BlockSpec(memory_space=pltpu.VMEM)
    hbm = pl.BlockSpec(memory_space=pl.ANY)
    n_gather = n_gy + 2 * n_y
    n_setup = 2 * n_y + n_gy
    dma = pltpu.SemaphoreType.DMA
    sol, res, norm = pl.pallas_call(
        functools.partial(kernel, n_gx, n_gy, corners),
        out_shape=(
            jax.ShapeDtypeStruct((order, loads), f32),
            jax.ShapeDtypeStruct((order, loads), f32),
            jax.ShapeDtypeStruct((ITERS, loads), f32),
        ),
        in_specs=[vmem, vmem, hbm, hbm, vmem],
        out_specs=(vmem, vmem, vmem),
        scratch_shapes=[
            pltpu.VMEM((order, order), bf16),
            pltpu.VMEM((rows_c, cols_c), f32),
            pltpu.VMEM((rows_c, cols_p), bf16),
            pltpu.VMEM((n_gx, n_gy * 8, 128), f32),
            pltpu.VMEM((n_gx, strip, 128), f32),
            pltpu.VMEM((n_gx, strip, cols_p), f32),
            pltpu.VMEM((n_y, strip, cols_p), f32),
            pltpu.VMEM((n_y, strip, cols_p), f32),
            pltpu.VMEM((n_gy, corners, cols_p), f32),
            pltpu.VMEM((n_gy, corners, cols_p), f32),
            pltpu.VMEM((corners, n_gx * strip), f32),
            pltpu.VMEM((order, loads), f32),
            pltpu.VMEM((order, loads), bf16),
            pltpu.VMEM((order, loads), bf16),
            pltpu.VMEM((ITERS, 4, side, loads), f32),
            pltpu.VMEM((ITERS, 4, side, loads), f32),
            pltpu.VMEM((ITERS, n_gx, strip, loads), f32),
            pltpu.VMEM((n_gy, 8, loads), f32),
            pltpu.VMEM((n_gx, 8, loads), f32),
            dma((2,)),
            dma((ITERS, 4)),
            dma((ITERS, 4)),
            dma((ITERS + 1, n_gather)),
            dma((ITERS + 1, n_gather)),
            dma((n_setup,)),
            dma((n_setup,)),
            dma((n_gy + n_gx,)),
            dma((n_gy + n_gx,)),
        ],
        compiler_params=pltpu.CompilerParams(
            collective_id=0, has_side_effects=True, vmem_limit_bytes=52 * 1024 * 1024
        ),
    )(right_side[0, 0].T, flex[0, 0], stiff[0, 0], coarse_inv, info)
    return (sol.T[None, None], res.T[None, None], norm)


def solution(mesh):
    placed = (
        P("gx", "gy", None, None),
        P("gx", "gy", None, None),
        P("gx", "gy", None, None),
        P("gx", "gy"),
        P("gx", "gy", None),
        P("gx", "gy", None),
    )
    return jax.shard_map(
        local,
        mesh=mesh,
        in_specs=placed,
        out_specs=(P("gx", "gy", None, None), P("gx", "gy", None, None), P()),
        check_vma=False,
    )
```

```python
import functools

import jax
import jax.numpy as jnp
from jax import lax
from jax.experimental import pallas as pl
from jax.experimental.pallas import tpu as pltpu
from jax.sharding import PartitionSpec as P

ITERS = 3

cheb_center = 1.15
cheb_half = 0.85
cheb_sigma = cheb_center / cheb_half

MESH = pl.DeviceIdType.MESH
OPP = (1, 0, 3, 2)


def remote(src, dst, send_sem, recv_sem, device):
    return pltpu.make_async_remote_copy(
        src_ref=src,
        dst_ref=dst,
        send_sem=send_sem,
        recv_sem=recv_sem,
        device_id=device,
        device_id_type=MESH,
    )


def kernel(
    n_gx, n_gy, corners, split, fold,
    rhs_ref, flex_ref, stiff_hbm, cinv_hbm, info_ref,
    sol_ref, res_ref, norm_ref,
    stiff_ref, cinv_ref, cbf_ref, info_all, ids_ref, part_ref, from_core, from_y, own_rows, from_gy, coarse_ref,
    dir_ref, dbf_ref, bal_ref, flexed_0, flexed_1, recv_0, recv_1, vals_0, vals_1, norm_gy, norm_gx,
    local_sem, side_send, side_recv, gat_send, gat_recv, set_send, set_recv, nrm_send, nrm_recv,
):
    row = lax.axis_index("gx")
    col = lax.axis_index("gy")
    core = lax.rem(row, 2)
    chip = lax.div(row, 2)
    n_y = n_gx // 2
    order, loads = dir_ref.shape
    side = order // 4
    n_sub = n_gx * n_gy
    rows_c, cols_c = cinv_ref.shape
    sibling = (chip * 2 + 1 - core, col)
    lanes = (slice(0, split), slice(split, loads))
    folds = (1, fold)
    flexed_refs, recv_refs, vals_refs = (flexed_0, flexed_1), (recv_0, recv_1), (vals_0, vals_1)
    pending = []

    def folded(x, h):
        n = folds[h]
        part = side // n
        return x if n == 1 else jnp.concatenate([x[i * part : (i + 1) * part] for i in range(n)], axis=1)

    def unfolded(x, h):
        n = folds[h]
        width = loads - split
        return x if n == 1 else jnp.concatenate([x[:, i * width : (i + 1) * width] for i in range(n)], axis=0)

    copy_stiff = pltpu.make_async_copy(stiff_hbm, stiff_ref, local_sem.at[0])
    copy_cinv = pltpu.make_async_copy(cinv_hbm, cinv_ref, local_sem.at[1])
    copy_stiff.start()
    copy_cinv.start()

    barrier = pltpu.get_barrier_semaphore()
    gy_peers = [(row, lax.rem(col + k, n_gy)) for k in range(1, n_gy)]
    gx_peers = [(lax.rem(row + k, n_gx), col) for k in range(1, n_gx)]
    for peer in gy_peers + gx_peers:
        pl.semaphore_signal(barrier, inc=1, device_id=peer, device_id_type=MESH)

    has = (col > 0, col < n_gy - 1, row > 0, row < n_gx - 1)
    neighbour = (
        (row, jnp.maximum(col - 1, 0)),
        (row, jnp.minimum(col + 1, n_gy - 1)),
        (jnp.maximum(row - 1, 0), col),
        (jnp.minimum(row + 1, n_gx - 1), col),
    )
    info_all[row, pl.ds(pl.multiple_of(col * 8, 8), 8)] = info_ref[...]
    turned = rhs_ref[...].T
    res_ref[...] = turned
    direction = turned * (1.0 / cheb_center)
    dir_ref[...] = direction
    sol_ref[...] = direction
    dbf_ref[...] = direction.astype(jnp.bfloat16)
    for s in range(4):
        @pl.when(jnp.logical_not(has[s]))
        def _():
            for it in range(ITERS):
                for ref in recv_refs:
                    ref[it, s] = jnp.zeros(ref.shape[2:], jnp.float32)

    pl.semaphore_wait(barrier, n_gy - 1 + n_gx - 1)

    def gather_start(buf, height, g):
        mine = buf.at[row, pl.ds(pl.multiple_of(col * height, 8), height)]
        copies = []
        for k in range(1, n_gy):
            c = remote(mine, mine, gat_send.at[g, k], gat_recv.at[g, k], gy_peers[k - 1])
            c.start()
            copies.append(c)
        pending.extend(copies)
        return copies

    def gather_across(buf, g, copies):
        for c in copies:
            c.wait_recv()
        base = n_gy
        slab = buf.at[row]
        across = []
        for j in range(1, n_y):
            peer = (lax.rem(chip + j, n_y) * 2 + core, col)
            c = remote(slab, slab, gat_send.at[g, base + j], gat_recv.at[g, base + j], peer)
            c.start()
            across.append(c)
        base = n_gy + n_y
        c = remote(slab, slab, gat_send.at[g, base], gat_recv.at[g, base], sibling)
        c.start()
        pending.extend(across + [c])
        return across, [c]

    def gather_twin(buf, g, state):
        across, twin = state
        base = n_gy + n_y
        for j in range(1, n_y):
            across[j - 1].wait_recv()
            arrived = buf.at[lax.rem(chip + n_y - j, n_y) * 2 + core]
            c = remote(arrived, arrived, gat_send.at[g, base + j], gat_recv.at[g, base + j], sibling)
            c.start()
            twin.append(c)
        pending.extend(twin[1:])
        return twin

    def gather_end(twin):
        for c in twin:
            c.wait_recv()

    def side_copy(it, h, s):
        return remote(
            flexed_refs[h].at[it, s], recv_refs[h].at[it, OPP[s]],
            side_send.at[it, h, s], side_recv.at[it, h, OPP[s]], neighbour[s],
        )

    def side_arrival(it, h, s):
        return remote(
            flexed_refs[h].at[it, s], recv_refs[h].at[it, s],
            side_send.at[it, h, s], side_recv.at[it, h, s], neighbour[s],
        )

    def flex_product(h, s, inner):
        return folded(
            jnp.dot(
                flex_ref[s * side : (s + 1) * side, inner], dbf_ref[inner, lanes[h]],
                preferred_element_type=jnp.float32,
            ),
            h,
        )

    def send_side(it, h, s):
        @pl.when(has[s])
        def _():
            side_copy(it, h, s).start()

    info_g = 2 * ITERS
    info_copies = gather_start(info_all, 8, info_g)

    for s in range(4):
        flexed_refs[0][0, s] = flex_product(0, s, slice(0, order))
        send_side(0, 0, s)

    copy_cinv.wait()
    if cbf_ref.shape[1] > cols_c:
        cbf_ref[...] = jnp.zeros(cbf_ref.shape, jnp.bfloat16)
    cbf_ref[:, 0:cols_c] = cinv_ref[...].astype(jnp.bfloat16)
    info_state = gather_across(info_all, info_g, info_copies)
    for s in range(4):
        flexed_refs[1][0, s] = flex_product(1, s, slice(0, order))
        send_side(0, 1, s)
    gather_end(gather_twin(info_all, info_g, info_state))

    lane = lax.broadcasted_iota(jnp.int32, (corners, 128), 1)
    sub = lax.broadcasted_iota(jnp.int32, (corners, 128), 0)
    for a in range(n_gx):
        for b in range(n_gy):
            line = jnp.broadcast_to(info_all[a, b * 8 : b * 8 + 1, :], (corners, 128))
            column = jnp.sum(jnp.where(lane == sub, line, 0.0), axis=1, keepdims=True)
            ids_ref[a, b * corners : (b + 1) * corners, :] = jnp.broadcast_to(column, (corners, 128))

    strip = n_gy * corners
    row_iota = lax.broadcasted_iota(jnp.int32, (strip, rows_c), 1).astype(jnp.float32)
    row_base = (row * rows_c).astype(jnp.float32)
    for a in range(n_gx):
        pick = jnp.where(ids_ref[a][:, 0:1] - row_base == row_iota, 1.0, 0.0).astype(jnp.bfloat16)
        part_ref[a] = jnp.dot(pick, cbf_ref[...], preferred_element_type=jnp.float32)
    to_core = []
    for j in range(n_y):
        c = remote(
            part_ref.at[2 * j + 1 - core], from_core.at[j], set_send.at[j], set_recv.at[j], sibling
        )
        c.start()
        to_core.append(c)
    pending.extend(to_core)

    def lines_at(a, b, entry):
        base = pl.multiple_of(b * 8, 8)
        return info_all[a, pl.ds(base, 8), :][1:2, entry : entry + 1]

    west_of = lax.rem(col + n_gy - 1, n_gy)
    north_of = lax.rem(row + n_gx - 1, n_gx)
    limits = (
        lines_at(row, west_of, 0) * jnp.where(has[0], 1.0, 0.0),
        lines_at(row, col, 0) * jnp.where(has[1], 1.0, 0.0),
        lines_at(north_of, col, 1) * jnp.where(has[2], 1.0, 0.0),
        lines_at(row, col, 1) * jnp.where(has[3], 1.0, 0.0),
    )

    def side_rows_of(h):
        shape = recv_refs[h].shape[2:]
        index = lax.broadcasted_iota(jnp.int32, shape, 0)
        at = lax.broadcasted_iota(jnp.int32, shape, 1)
        for i in range(1, folds[h]):
            index = index + jnp.where(at >= i * (loads - split), side // folds[h], 0)
        return index.astype(jnp.float32)

    side_iota = (side_rows_of(0), side_rows_of(1))

    for c in to_core:
        c.wait_recv()
    to_y = []
    for j in range(1, n_y):
        target = lax.rem(chip + j, n_y)
        from_core[target] = from_core[target] + part_ref[2 * target + core]
        c = remote(
            from_core.at[target], from_y.at[j - 1], set_send.at[n_y + j - 1], set_recv.at[n_y + j - 1],
            (target * 2 + core, col),
        )
        c.start()
        to_y.append(c)
    pending.extend(to_y)

    def set_spread():
        own_strip = from_core[chip] + part_ref[2 * chip + core]
        for j in range(1, n_y):
            to_y[j - 1].wait_recv()
            own_strip = own_strip + from_y[j - 1]
        for b in range(n_gy):
            own_rows[b] = own_strip[b * corners : (b + 1) * corners]
        base = 2 * n_y
        from_gy[col] = own_rows[col]
        to_gy = []
        for k in range(1, n_gy):
            c = remote(
                own_rows.at[lax.rem(col + k, n_gy)], from_gy.at[col],
                set_send.at[base + k], set_recv.at[base + k], gy_peers[k - 1],
            )
            c.start()
            to_gy.append(c)
        pending.extend(to_gy)
        return to_gy

    def set_finish(to_gy):
        for c in to_gy:
            c.wait_recv()
        col_iota = lax.broadcasted_iota(jnp.int32, (strip, cbf_ref.shape[1]), 1).astype(jnp.float32)
        strips = []
        for a in range(n_gx):
            def add(b, total):
                base_col = (b * cols_c).astype(jnp.float32)
                pick = jnp.where(ids_ref[a][:, 0:1] - base_col == col_iota, 1.0, 0.0).astype(jnp.bfloat16)
                return total + lax.dot_general(
                    from_gy[b].astype(jnp.bfloat16), pick, (((1,), (1,)), ((), ())),
                    preferred_element_type=jnp.float32,
                )

            strips.append(lax.fori_loop(0, n_gy, add, jnp.zeros((corners, strip), jnp.float32)))
        coarse_ref[...] = jnp.concatenate(strips, axis=1)

    copy_stiff.wait()

    rho_prev = 1.0 / cheb_sigma
    for it in range(ITERS):
        last = it + 1 == ITERS
        if not last:
            rho_next = 1.0 / (2.0 * cheb_sigma - rho_prev)
            keep, gain = rho_next * rho_prev, 2.0 * rho_next / cheb_half
            rho_prev = rho_next

        def balance(h):
            for s in (2, 3, 0, 1):
                @pl.when(has[s])
                def _():
                    side_arrival(it, h, s).wait_recv()

                own = flexed_refs[h][it, s]
                jump = jnp.where(side_iota[h] < limits[s], recv_refs[h][it, s] - own, 0.0)
                bal_ref[s * side : (s + 1) * side, lanes[h]] = unfolded(own + 0.5 * jump, h).astype(jnp.bfloat16)

        def head_part(h):
            head = jnp.dot(stiff_ref[0:32, :], bal_ref[:, lanes[h]], preferred_element_type=jnp.float32)
            vals_refs[h][it, row, pl.ds(pl.multiple_of(col * corners, 8), corners)] = head[0:corners]
            return head, gather_start(vals_refs[h].at[it], corners, 2 * it + h)

        def rest_part(h, head):
            at = lanes[h]
            rest = jnp.dot(stiff_ref[32:, :], bal_ref[:, at], preferred_element_type=jnp.float32)
            mid = res_ref[corners:32, at] - head[corners:]
            low = res_ref[32:, at] - rest
            res_ref[corners:32, at] = mid
            res_ref[32:, at] = low
            squares = jnp.sum(low * low, axis=0, keepdims=True) + jnp.sum(mid * mid, axis=0, keepdims=True)
            if not last:
                later = keep * dir_ref[corners:, at] + gain * res_ref[corners:, at]
                dir_ref[corners:, at] = later
                sol_ref[corners:, at] = sol_ref[corners:, at] + later
                dbf_ref[128:, at] = later[128 - corners :].astype(jnp.bfloat16)
            return squares

        def flex_main(h):
            if not last:
                for s in range(4):
                    flexed_refs[h][it + 1, s] = flex_product(h, s, slice(128, order))

        def correct(h, head, squares):
            at = lanes[h]
            fixed = head[0:corners] + jnp.dot(
                coarse_ref[...].astype(jnp.bfloat16),
                vals_refs[h][it].reshape(n_sub * corners, vals_refs[h].shape[3]).astype(jnp.bfloat16),
                preferred_element_type=jnp.float32,
            )
            top = res_ref[0:corners, at] - fixed
            res_ref[0:corners, at] = top
            norm_gy[col, it : it + 1, at] = squares + jnp.sum(top * top, axis=0, keepdims=True)
            if not last:
                later = keep * dir_ref[0:corners, at] + gain * top
                dir_ref[0:corners, at] = later
                sol_ref[0:corners, at] = sol_ref[0:corners, at] + later
                dbf_ref[0:128, at] = dir_ref[0:128, at].astype(jnp.bfloat16)
                for s in range(4):
                    flexed_refs[h][it + 1, s] += flex_product(h, s, slice(0, 128))
                    send_side(it + 1, h, s)

        bufs = (vals_0.at[it], vals_1.at[it])
        balance(0)
        head_0, copies_0 = head_part(0)
        squares_0 = rest_part(0, head_0)
        if it == 0:
            to_gy = set_spread()
        balance(1)
        head_1, copies_1 = head_part(1)
        state_0 = gather_across(bufs[0], 2 * it, copies_0)
        flex_main(0)
        twin_0 = gather_twin(bufs[0], 2 * it, state_0)
        squares_1 = rest_part(1, head_1)
        state_1 = gather_across(bufs[1], 2 * it + 1, copies_1)
        if it == 0:
            set_finish(to_gy)
        gather_end(twin_0)
        correct(0, head_0, squares_0)
        flex_main(1)
        twin_1 = gather_twin(bufs[1], 2 * it + 1, state_1)
        gather_end(twin_1)
        correct(1, head_1, squares_1)

    mine = norm_gy.at[col]
    sums = []
    for k in range(1, n_gy):
        c = remote(mine, mine, nrm_send.at[k], nrm_recv.at[k], gy_peers[k - 1])
        c.start()
        sums.append(c)
    for c in sums:
        c.wait_recv()
    total = norm_gy[0, 0:ITERS]
    for b in range(1, n_gy):
        total = total + norm_gy[b, 0:ITERS]
    norm_gx[row, 0:ITERS] = total
    mine = norm_gx.at[row]
    wide = []
    for k in range(1, n_gx):
        c = remote(mine, mine, nrm_send.at[n_gy + k], nrm_recv.at[n_gy + k], gx_peers[k - 1])
        c.start()
        wide.append(c)
    for c in wide:
        c.wait_recv()
    total = norm_gx[0, 0:ITERS]
    for a in range(1, n_gx):
        total = total + norm_gx[a, 0:ITERS]
    norm_ref[...] = jnp.sqrt(total / (n_sub * order))

    for c in pending + sums + wide:
        c.wait_send()
    for s in range(4):
        @pl.when(has[s])
        def _():
            for it in range(ITERS):
                for h in range(2):
                    side_copy(it, h, s).wait_send()


def local(right_side, flex, stiff, coarse_inv, corner_map, side_rows):
    n_gx = lax.axis_size("gx")
    n_gy = lax.axis_size("gy")
    n_y = n_gx // 2
    loads, order = right_side.shape[2:]
    corners = corner_map.shape[2]
    side = order // 4
    rows_c, cols_c = coarse_inv.shape
    strip = n_gy * corners
    split = 128
    width = loads - split
    fold = 2 if 2 * width <= 128 else 1
    cols_p = -(-cols_c // 128) * 128
    info = jnp.concatenate(
        [
            jnp.pad(corner_map[0].astype(jnp.float32), ((0, 0), (0, 128 - corners))),
            jnp.pad(side_rows[0].astype(jnp.float32), ((0, 6), (0, 126))),
        ]
    )
    f32, bf16 = jnp.float32, jnp.bfloat16
    vmem = pl.BlockSpec(memory_space=pltpu.VMEM)
    hbm = pl.BlockSpec(memory_space=pl.ANY)
    n_gather = n_gy + 2 * n_y
    n_setup = 2 * n_y + n_gy
    dma = pltpu.SemaphoreType.DMA
    sol, res, norm = pl.pallas_call(
        functools.partial(kernel, n_gx, n_gy, corners, split, fold),
        out_shape=(
            jax.ShapeDtypeStruct((order, loads), f32),
            jax.ShapeDtypeStruct((order, loads), f32),
            jax.ShapeDtypeStruct((ITERS, loads), f32),
        ),
        in_specs=[vmem, vmem, hbm, hbm, vmem],
        out_specs=(vmem, vmem, vmem),
        scratch_shapes=[
            pltpu.VMEM((order, order), bf16),
            pltpu.VMEM((rows_c, cols_c), f32),
            pltpu.VMEM((rows_c, cols_p), bf16),
            pltpu.VMEM((n_gx, n_gy * 8, 128), f32),
            pltpu.VMEM((n_gx, strip, 128), f32),
            pltpu.VMEM((n_gx, strip, cols_p), f32),
            pltpu.VMEM((n_y, strip, cols_p), f32),
            pltpu.VMEM((n_y, strip, cols_p), f32),
            pltpu.VMEM((n_gy, corners, cols_p), f32),
            pltpu.VMEM((n_gy, corners, cols_p), f32),
            pltpu.VMEM((corners, n_gx * strip), f32),
            pltpu.VMEM((order, loads), f32),
            pltpu.VMEM((order, loads), bf16),
            pltpu.VMEM((order, loads), bf16),
            pltpu.VMEM((ITERS, 4, side, split), f32),
            pltpu.VMEM((ITERS, 4, side // fold, width * fold), f32),
            pltpu.VMEM((ITERS, 4, side, split), f32),
            pltpu.VMEM((ITERS, 4, side // fold, width * fold), f32),
            pltpu.VMEM((ITERS, n_gx, strip, split), f32),
            pltpu.VMEM((ITERS, n_gx, strip, width), f32),
            pltpu.VMEM((n_gy, 8, loads), f32),
            pltpu.VMEM((n_gx, 8, loads), f32),
            dma((2,)),
            dma((ITERS, 2, 4)),
            dma((ITERS, 2, 4)),
            dma((2 * ITERS + 1, n_gather)),
            dma((2 * ITERS + 1, n_gather)),
            dma((n_setup,)),
            dma((n_setup,)),
            dma((n_gy + n_gx,)),
            dma((n_gy + n_gx,)),
        ],
        compiler_params=pltpu.CompilerParams(
            collective_id=0, has_side_effects=True, vmem_limit_bytes=52 * 1024 * 1024
        ),
    )(right_side[0, 0], flex[0, 0], stiff[0, 0], coarse_inv, info)
    return (sol.T[None, None], res.T[None, None], norm)


def solution(mesh):
    placed = (
        P("gx", "gy", None, None),
        P("gx", "gy", None, None),
        P("gx", "gy", None, None),
        P("gx", "gy"),
        P("gx", "gy", None),
        P("gx", "gy", None),
    )
    return jax.shard_map(
        local,
        mesh=mesh,
        in_specs=placed,
        out_specs=(P("gx", "gy", None, None), P("gx", "gy", None, None), P()),
        check_vma=False,
    )
```

```python
import functools

import jax
import jax.numpy as jnp
from jax import lax
from jax.experimental import pallas as pl
from jax.experimental.pallas import tpu as pltpu
from jax.sharding import PartitionSpec as P

ITERS = 3

cheb_center = 1.15
cheb_half = 0.85
cheb_sigma = cheb_center / cheb_half

MESH = pl.DeviceIdType.MESH
OPP = (1, 0, 3, 2)


def remote(src, dst, send_sem, recv_sem, device):
    return pltpu.make_async_remote_copy(
        src_ref=src,
        dst_ref=dst,
        send_sem=send_sem,
        recv_sem=recv_sem,
        device_id=device,
        device_id_type=MESH,
    )


def kernel(
    n_gx, n_gy, corners, split, fold,
    rhs_ref, flex_ref, stiff_hbm, cinv_hbm, map_ref, count_ref,
    sol_ref, res_ref, norm_ref,
    stiff_ref, cinv_ref, cbf_ref, info_ref, info_all, ids_ref, part_ref, from_core, from_y, own_rows, from_gy, coarse_ref, sel_ref, sum_ref, left_ref,
    dir_ref, dbf_ref, bal_ref, flexed_0, flexed_1, recv_0, recv_1, vals_0, vals_1, norm_gy, norm_gx,
    local_sem, side_send, side_recv, gat_send, gat_recv, set_send, set_recv, nrm_send, nrm_recv,
):
    row = lax.axis_index("gx")
    col = lax.axis_index("gy")
    core = lax.rem(row, 2)
    chip = lax.div(row, 2)
    n_y = n_gx // 2
    order, loads = dir_ref.shape
    side = order // 4
    n_sub = n_gx * n_gy
    rows_c, cols_c = cinv_ref.shape
    sibling = (chip * 2 + 1 - core, col)
    lanes = (slice(0, split), slice(split, loads))
    folds = (1, fold)
    flexed_refs, recv_refs, vals_refs = (flexed_0, flexed_1), (recv_0, recv_1), (vals_0, vals_1)
    pending = []

    def folded(x, h):
        n = folds[h]
        part = side // n
        return x if n == 1 else jnp.concatenate([x[i * part : (i + 1) * part] for i in range(n)], axis=1)

    def unfolded(x, h):
        n = folds[h]
        width = loads - split
        return x if n == 1 else jnp.concatenate([x[:, i * width : (i + 1) * width] for i in range(n)], axis=0)

    copy_stiff = pltpu.make_async_copy(stiff_hbm, stiff_ref, local_sem.at[0])
    copy_cinv = pltpu.make_async_copy(cinv_hbm, cinv_ref, local_sem.at[1])
    copy_stiff.start()
    copy_cinv.start()

    barrier = pltpu.get_barrier_semaphore()
    gy_peers = [(row, lax.rem(col + k, n_gy)) for k in range(1, n_gy)]
    gx_peers = [(lax.rem(row + k, n_gx), col) for k in range(1, n_gx)]
    for peer in gy_peers + gx_peers:
        pl.semaphore_signal(barrier, inc=1, device_id=peer, device_id_type=MESH)

    has = (col > 0, col < n_gy - 1, row > 0, row < n_gx - 1)
    neighbour = (
        (row, jnp.maximum(col - 1, 0)),
        (row, jnp.minimum(col + 1, n_gy - 1)),
        (jnp.maximum(row - 1, 0), col),
        (jnp.minimum(row + 1, n_gx - 1), col),
    )
    info_ref[...] = jnp.zeros(info_ref.shape, jnp.float32)
    info_ref[0:1, 0:corners] = map_ref[...].astype(jnp.float32)
    info_ref[1:2, 0:2] = count_ref[...].astype(jnp.float32)
    info_all[row, pl.ds(pl.multiple_of(col * 8, 8), 8)] = info_ref[...]
    turned = rhs_ref[...].T
    left_ref[...] = turned
    direction = turned * (1.0 / cheb_center)
    dir_ref[...] = direction
    sum_ref[...] = direction
    dbf_ref[...] = direction.astype(jnp.bfloat16)
    for s in range(4):
        @pl.when(jnp.logical_not(has[s]))
        def _():
            for it in range(ITERS):
                for ref in recv_refs:
                    ref[it, s] = jnp.zeros(ref.shape[2:], jnp.float32)

    pl.semaphore_wait(barrier, n_gy - 1 + n_gx - 1)

    def gather_start(buf, height, g):
        mine = buf.at[row, pl.ds(pl.multiple_of(col * height, 8), height)]
        copies = []
        for k in range(1, n_gy):
            c = remote(mine, mine, gat_send.at[g, k], gat_recv.at[g, k], gy_peers[k - 1])
            c.start()
            copies.append(c)
        pending.extend(copies)
        return copies

    def gather_across(buf, g, copies):
        for c in copies:
            c.wait_recv()
        base = n_gy
        slab = buf.at[row]
        across = []
        for j in range(1, n_y):
            peer = (lax.rem(chip + j, n_y) * 2 + core, col)
            c = remote(slab, slab, gat_send.at[g, base + j], gat_recv.at[g, base + j], peer)
            c.start()
            across.append(c)
        base = n_gy + n_y
        c = remote(slab, slab, gat_send.at[g, base], gat_recv.at[g, base], sibling)
        c.start()
        pending.extend(across + [c])
        return across, [c]

    def gather_twin(buf, g, state):
        across, twin = state
        base = n_gy + n_y
        for j in range(1, n_y):
            across[j - 1].wait_recv()
            arrived = buf.at[lax.rem(chip + n_y - j, n_y) * 2 + core]
            c = remote(arrived, arrived, gat_send.at[g, base + j], gat_recv.at[g, base + j], sibling)
            c.start()
            twin.append(c)
        pending.extend(twin[1:])
        return twin

    def gather_end(twin):
        for c in twin:
            c.wait_recv()

    def side_copy(it, h, s):
        return remote(
            flexed_refs[h].at[it, s], recv_refs[h].at[it, OPP[s]],
            side_send.at[it, h, s], side_recv.at[it, h, OPP[s]], neighbour[s],
        )

    def side_arrival(it, h, s):
        return remote(
            flexed_refs[h].at[it, s], recv_refs[h].at[it, s],
            side_send.at[it, h, s], side_recv.at[it, h, s], neighbour[s],
        )

    def flex_product(h, s, inner):
        return folded(
            jnp.dot(
                flex_ref[s * side : (s + 1) * side, inner], dbf_ref[inner, lanes[h]],
                preferred_element_type=jnp.float32,
            ),
            h,
        )

    def send_side(it, h, s):
        @pl.when(has[s])
        def _():
            side_copy(it, h, s).start()

    info_g = 2 * ITERS
    info_copies = gather_start(info_all, 8, info_g)

    for s in range(4):
        flexed_refs[0][0, s] = flex_product(0, s, slice(0, order))
        send_side(0, 0, s)

    copy_cinv.wait()
    if cbf_ref.shape[1] > cols_c:
        cbf_ref[...] = jnp.zeros(cbf_ref.shape, jnp.bfloat16)
    cbf_ref[:, 0:cols_c] = cinv_ref[...].astype(jnp.bfloat16)
    info_state = gather_across(info_all, info_g, info_copies)
    for s in range(4):
        flexed_refs[1][0, s] = flex_product(1, s, slice(0, order))
        send_side(0, 1, s)
    gather_end(gather_twin(info_all, info_g, info_state))

    lane = lax.broadcasted_iota(jnp.int32, (corners, 128), 1)
    sub = lax.broadcasted_iota(jnp.int32, (corners, 128), 0)
    for a in range(n_gx):
        for b in range(n_gy):
            line = jnp.broadcast_to(info_all[a, b * 8 : b * 8 + 1, :], (corners, 128))
            column = jnp.sum(jnp.where(lane == sub, line, 0.0), axis=1, keepdims=True)
            ids_ref[a, b * corners : (b + 1) * corners, :] = jnp.broadcast_to(column, (corners, 128))

    strip = n_gy * corners
    row_iota = lax.broadcasted_iota(jnp.int32, (strip, rows_c), 1).astype(jnp.float32)
    to_core = []
    row_base = (row * rows_c).astype(jnp.float32)
    for a in range(n_gx):
        pick = jnp.where(ids_ref[a][:, 0:1] - row_base == row_iota, 1.0, 0.0).astype(jnp.bfloat16)
        part_ref[a] = jnp.dot(pick, cbf_ref[...], preferred_element_type=jnp.float32)
        if a % 2 == 1:
            j = a // 2
            c = remote(
                part_ref.at[2 * j + 1 - core], from_core.at[j], set_send.at[j], set_recv.at[j], sibling
            )
            c.start()
            to_core.append(c)
    pending.extend(to_core)

    def lines_at(a, b, entry):
        base = pl.multiple_of(b * 8, 8)
        return info_all[a, pl.ds(base, 8), :][1:2, entry : entry + 1]

    west_of = lax.rem(col + n_gy - 1, n_gy)
    north_of = lax.rem(row + n_gx - 1, n_gx)
    limits = (
        lines_at(row, west_of, 0) * jnp.where(has[0], 1.0, 0.0),
        lines_at(row, col, 0) * jnp.where(has[1], 1.0, 0.0),
        lines_at(north_of, col, 1) * jnp.where(has[2], 1.0, 0.0),
        lines_at(row, col, 1) * jnp.where(has[3], 1.0, 0.0),
    )

    def side_rows_of(h):
        shape = recv_refs[h].shape[2:]
        index = lax.broadcasted_iota(jnp.int32, shape, 0)
        at = lax.broadcasted_iota(jnp.int32, shape, 1)
        for i in range(1, folds[h]):
            index = index + jnp.where(at >= i * (loads - split), side // folds[h], 0)
        return index.astype(jnp.float32)

    side_iota = (side_rows_of(0), side_rows_of(1))

    for c in to_core:
        c.wait_recv()
    chunks = 2
    per_chunk = n_gy // chunks
    span = per_chunk * corners
    to_y = [[] for _ in range(chunks)]
    for j in range(1, n_y):
        target = lax.rem(chip + j, n_y)
        from_core[target] = from_core[target] + part_ref[2 * target + core]
        for q in range(chunks):
            rows_q = pl.ds(q * span, span)
            at = n_y + (j - 1) * chunks + q
            c = remote(
                from_core.at[target, rows_q], from_y.at[j - 1, rows_q], set_send.at[at], set_recv.at[at],
                (target * 2 + core, col),
            )
            c.start()
            to_y[q].append(c)
    for q in range(chunks):
        pending.extend(to_y[q])

    coarse = n_gy * cols_c
    col_iota = lax.broadcasted_iota(jnp.int32, (strip, coarse), 1).astype(jnp.float32)
    for a in range(n_gx):
        sel_ref[a * strip : (a + 1) * strip, :] = jnp.where(ids_ref[a][:, 0:1] == col_iota, 1.0, 0.0).astype(
            jnp.bfloat16
        )
    gy_base = n_y + (n_y - 1) * chunks

    def own_copy(b):
        return remote(
            own_rows.at[b], from_gy.at[col], set_send.at[gy_base + b], set_recv.at[gy_base + col], (row, b)
        )

    def own_arrival(b):
        return remote(
            own_rows.at[b], from_gy.at[b], set_send.at[gy_base + b], set_recv.at[gy_base + b], (row, b)
        )

    def set_spread(q):
        rows_q = slice(q * span, (q + 1) * span)
        own_strip = from_core[chip, rows_q] + part_ref[2 * chip + core, rows_q]
        for j in range(1, n_y):
            to_y[q][j - 1].wait_recv()
            own_strip = own_strip + from_y[j - 1, rows_q]
        for i in range(per_chunk):
            b = q * per_chunk + i
            own_rows[b] = own_strip[i * corners : (i + 1) * corners]

            @pl.when(b != col)
            def _():
                own_copy(b).start()

            @pl.when(b == col)
            def _():
                from_gy[b] = own_rows[b]

    def set_finish():
        for b in range(n_gy):
            @pl.when(b != col)
            def _():
                own_arrival(b).wait_recv()

        held = jnp.concatenate([from_gy[b][:, 0:cols_c] for b in range(n_gy)], axis=1).astype(jnp.bfloat16)
        coarse_ref[...] = lax.dot_general(
            held, sel_ref[...], (((1,), (1,)), ((), ())), preferred_element_type=jnp.float32
        )

    copy_stiff.wait()

    rho_prev = 1.0 / cheb_sigma
    for it in range(ITERS):
        last = it + 1 == ITERS
        if not last:
            rho_next = 1.0 / (2.0 * cheb_sigma - rho_prev)
            keep, gain = rho_next * rho_prev, 2.0 * rho_next / cheb_half
            rho_prev = rho_next

        def balance(h):
            for s in (2, 3, 0, 1):
                @pl.when(has[s])
                def _():
                    side_arrival(it, h, s).wait_recv()

                own = flexed_refs[h][it, s]
                jump = jnp.where(side_iota[h] < limits[s], recv_refs[h][it, s] - own, 0.0)
                bal_ref[s * side : (s + 1) * side, lanes[h]] = unfolded(own + 0.5 * jump, h).astype(jnp.bfloat16)

        def head_part(h):
            head = jnp.dot(stiff_ref[0:32, :], bal_ref[:, lanes[h]], preferred_element_type=jnp.float32)
            vals_refs[h][it, row, pl.ds(pl.multiple_of(col * corners, 8), corners)] = head[0:corners]
            return head, gather_start(vals_refs[h].at[it], corners, 2 * it + h)

        def rest_part(h, head):
            at = lanes[h]
            rest = jnp.dot(stiff_ref[32:, :], bal_ref[:, at], preferred_element_type=jnp.float32)
            mid = left_ref[corners:32, at] - head[corners:]
            low = left_ref[32:, at] - rest
            left_ref[corners:32, at] = mid
            left_ref[32:, at] = low
            squares = jnp.sum(low * low, axis=0, keepdims=True) + jnp.sum(mid * mid, axis=0, keepdims=True)
            if not last:
                later = keep * dir_ref[corners:, at] + gain * left_ref[corners:, at]
                dir_ref[corners:, at] = later
                sum_ref[corners:, at] = sum_ref[corners:, at] + later
                dbf_ref[128:, at] = later[128 - corners :].astype(jnp.bfloat16)
            return squares

        def flex_main(h):
            if not last:
                for s in range(4):
                    flexed_refs[h][it + 1, s] = flex_product(h, s, slice(128, order))

        def correct(h, head, squares):
            at = lanes[h]
            fixed = head[0:corners] + jnp.dot(
                coarse_ref[...].astype(jnp.bfloat16),
                vals_refs[h][it].reshape(n_sub * corners, vals_refs[h].shape[3]).astype(jnp.bfloat16),
                preferred_element_type=jnp.float32,
            )
            top = left_ref[0:corners, at] - fixed
            left_ref[0:corners, at] = top
            norm_gy[col, it : it + 1, at] = squares + jnp.sum(top * top, axis=0, keepdims=True)
            if not last:
                later = keep * dir_ref[0:corners, at] + gain * top
                dir_ref[0:corners, at] = later
                sum_ref[0:corners, at] = sum_ref[0:corners, at] + later
                dbf_ref[0:128, at] = dir_ref[0:128, at].astype(jnp.bfloat16)
                for s in range(4):
                    flexed_refs[h][it + 1, s] += flex_product(h, s, slice(0, 128))
                    send_side(it + 1, h, s)

        bufs = (vals_0.at[it], vals_1.at[it])
        if last:
            sol_ref[...] = sum_ref[...].T
        balance(0)
        head_0, copies_0 = head_part(0)
        squares_0 = rest_part(0, head_0)
        if it == 0:
            for q in range(chunks):
                set_spread(q)
        balance(1)
        head_1, copies_1 = head_part(1)
        state_0 = gather_across(bufs[0], 2 * it, copies_0)
        flex_main(0)
        twin_0 = gather_twin(bufs[0], 2 * it, state_0)
        squares_1 = rest_part(1, head_1)
        state_1 = gather_across(bufs[1], 2 * it + 1, copies_1)
        if it == 0:
            set_finish()
        gather_end(twin_0)
        correct(0, head_0, squares_0)
        flex_main(1)
        twin_1 = gather_twin(bufs[1], 2 * it + 1, state_1)
        gather_end(twin_1)
        correct(1, head_1, squares_1)

    mine = norm_gy.at[col]
    sums = []
    for k in range(1, n_gy):
        c = remote(mine, mine, nrm_send.at[k], nrm_recv.at[k], gy_peers[k - 1])
        c.start()
        sums.append(c)
    res_ref[...] = left_ref[...].T
    for c in sums:
        c.wait_recv()
    total = norm_gy[0, 0:ITERS]
    for b in range(1, n_gy):
        total = total + norm_gy[b, 0:ITERS]
    norm_gx[row, 0:ITERS] = total
    mine = norm_gx.at[row]
    wide = []
    for k in range(1, n_gx):
        c = remote(mine, mine, nrm_send.at[n_gy + k], nrm_recv.at[n_gy + k], gx_peers[k - 1])
        c.start()
        wide.append(c)
    for c in wide:
        c.wait_recv()
    total = norm_gx[0, 0:ITERS]
    for a in range(1, n_gx):
        total = total + norm_gx[a, 0:ITERS]
    norm_ref[...] = jnp.sqrt(total / (n_sub * order))

    for c in pending + sums + wide:
        c.wait_send()
    for b in range(n_gy):
        @pl.when(b != col)
        def _():
            own_copy(b).wait_send()

    for s in range(4):
        @pl.when(has[s])
        def _():
            for it in range(ITERS):
                for h in range(2):
                    side_copy(it, h, s).wait_send()


def local(right_side, flex, stiff, coarse_inv, corner_map, side_rows):
    n_gx = lax.axis_size("gx")
    n_gy = lax.axis_size("gy")
    n_y = n_gx // 2
    loads, order = right_side.shape[2:]
    corners = corner_map.shape[2]
    side = order // 4
    rows_c, cols_c = coarse_inv.shape
    strip = n_gy * corners
    split = 128
    width = loads - split
    fold = 2 if 2 * width <= 128 else 1
    cols_p = -(-cols_c // 128) * 128
    f32, bf16 = jnp.float32, jnp.bfloat16
    vmem = pl.BlockSpec(memory_space=pltpu.VMEM)
    hbm = pl.BlockSpec(memory_space=pl.ANY)
    n_gather = n_gy + 2 * n_y
    n_setup = 3 * n_y + n_gy
    dma = pltpu.SemaphoreType.DMA
    sol, res, norm = pl.pallas_call(
        functools.partial(kernel, n_gx, n_gy, corners, split, fold),
        out_shape=(
            jax.ShapeDtypeStruct((loads, order), f32),
            jax.ShapeDtypeStruct((loads, order), f32),
            jax.ShapeDtypeStruct((ITERS, loads), f32),
        ),
        in_specs=[vmem, vmem, hbm, hbm, vmem, vmem],
        out_specs=(vmem, vmem, vmem),
        scratch_shapes=[
            pltpu.VMEM((order, order), bf16),
            pltpu.VMEM((rows_c, cols_c), f32),
            pltpu.VMEM((rows_c, cols_p), bf16),
            pltpu.VMEM((8, 128), f32),
            pltpu.VMEM((n_gx, n_gy * 8, 128), f32),
            pltpu.VMEM((n_gx, strip, 128), f32),
            pltpu.VMEM((n_gx, strip, cols_p), f32),
            pltpu.VMEM((n_y, strip, cols_p), f32),
            pltpu.VMEM((n_y, strip, cols_p), f32),
            pltpu.VMEM((n_gy, corners, cols_p), f32),
            pltpu.VMEM((n_gy, corners, cols_p), f32),
            pltpu.VMEM((corners, n_gx * strip), f32),
            pltpu.VMEM((n_gx * strip, n_gy * cols_c), bf16),
            pltpu.VMEM((order, loads), f32),
            pltpu.VMEM((order, loads), f32),
            pltpu.VMEM((order, loads), f32),
            pltpu.VMEM((order, loads), bf16),
            pltpu.VMEM((order, loads), bf16),
            pltpu.VMEM((ITERS, 4, side, split), f32),
            pltpu.VMEM((ITERS, 4, side // fold, width * fold), f32),
            pltpu.VMEM((ITERS, 4, side, split), f32),
            pltpu.VMEM((ITERS, 4, side // fold, width * fold), f32),
            pltpu.VMEM((ITERS, n_gx, strip, split), f32),
            pltpu.VMEM((ITERS, n_gx, strip, width), f32),
            pltpu.VMEM((n_gy, 8, loads), f32),
            pltpu.VMEM((n_gx, 8, loads), f32),
            dma((2,)),
            dma((ITERS, 2, 4)),
            dma((ITERS, 2, 4)),
            dma((2 * ITERS + 1, n_gather)),
            dma((2 * ITERS + 1, n_gather)),
            dma((n_setup,)),
            dma((n_setup,)),
            dma((n_gy + n_gx,)),
            dma((n_gy + n_gx,)),
        ],
        compiler_params=pltpu.CompilerParams(
            collective_id=0, has_side_effects=True, vmem_limit_bytes=57 * 1024 * 1024
        ),
    )(right_side[0, 0], flex[0, 0], stiff[0, 0], coarse_inv, corner_map[0], side_rows[0])
    return (sol[None, None], res[None, None], norm)


def solution(mesh):
    placed = (
        P("gx", "gy", None, None),
        P("gx", "gy", None, None),
        P("gx", "gy", None, None),
        P("gx", "gy"),
        P("gx", "gy", None),
        P("gx", "gy", None),
    )
    return jax.shard_map(
        local,
        mesh=mesh,
        in_specs=placed,
        out_specs=(P("gx", "gy", None, None), P("gx", "gy", None, None), P()),
        check_vma=False,
    )
```

```python
import functools

import jax
import jax.numpy as jnp
from jax import lax
from jax.experimental import pallas as pl
from jax.experimental.pallas import tpu as pltpu
from jax.sharding import PartitionSpec as P

ITERS = 3

cheb_center = 1.15
cheb_half = 0.85
cheb_sigma = cheb_center / cheb_half

MESH = pl.DeviceIdType.MESH
OPP = (1, 0, 3, 2)


def remote(src, dst, send_sem, recv_sem, device):
    return pltpu.make_async_remote_copy(
        src_ref=src,
        dst_ref=dst,
        send_sem=send_sem,
        recv_sem=recv_sem,
        device_id=device,
        device_id_type=MESH,
    )


def kernel(
    n_gx, n_gy, corners, split, fold,
    rhs_ref, flex_ref, stiff_hbm, cinv_hbm, map_ref, count_ref,
    sol_ref, res_ref, norm_ref,
    stiff_ref, cinv_ref, cbf_ref, info_ref, info_all, ids_ref, part_ref, from_core, from_y, own_rows, from_gy, coarse_ref, sel_ref,
    dir_ref, dbf_ref, bal_ref, flexed_0, flexed_1, recv_0, recv_1, vals_0, vals_1, norm_gy, norm_gx,
    local_sem, side_send, side_recv, gat_send, gat_recv, set_send, set_recv, nrm_send, nrm_recv,
):
    row = lax.axis_index("gx")
    col = lax.axis_index("gy")
    core = lax.rem(row, 2)
    chip = lax.div(row, 2)
    n_y = n_gx // 2
    order, loads = dir_ref.shape
    side = order // 4
    n_sub = n_gx * n_gy
    rows_c, cols_c = cinv_ref.shape
    sibling = (chip * 2 + 1 - core, col)
    lanes = (slice(0, split), slice(split, loads))
    folds = (1, fold)
    flexed_refs, recv_refs, vals_refs = (flexed_0, flexed_1), (recv_0, recv_1), (vals_0, vals_1)
    pending = []

    def folded(x, h):
        n = folds[h]
        part = side // n
        return x if n == 1 else jnp.concatenate([x[i * part : (i + 1) * part] for i in range(n)], axis=1)

    def unfolded(x, h):
        n = folds[h]
        width = loads - split
        return x if n == 1 else jnp.concatenate([x[:, i * width : (i + 1) * width] for i in range(n)], axis=0)

    copy_stiff = pltpu.make_async_copy(stiff_hbm, stiff_ref, local_sem.at[0])
    copy_cinv = pltpu.make_async_copy(cinv_hbm, cinv_ref, local_sem.at[1])
    copy_stiff.start()
    copy_cinv.start()

    barrier = pltpu.get_barrier_semaphore()
    gy_peers = [(row, lax.rem(col + k, n_gy)) for k in range(1, n_gy)]
    gx_peers = [(lax.rem(row + k, n_gx), col) for k in range(1, n_gx)]
    for peer in gy_peers + gx_peers:
        pl.semaphore_signal(barrier, inc=1, device_id=peer, device_id_type=MESH)

    has = (col > 0, col < n_gy - 1, row > 0, row < n_gx - 1)
    neighbour = (
        (row, jnp.maximum(col - 1, 0)),
        (row, jnp.minimum(col + 1, n_gy - 1)),
        (jnp.maximum(row - 1, 0), col),
        (jnp.minimum(row + 1, n_gx - 1), col),
    )
    info_ref[...] = jnp.zeros(info_ref.shape, jnp.float32)
    info_ref[0:1, 0:corners] = map_ref[...].astype(jnp.float32)
    info_ref[1:2, 0:2] = count_ref[...].astype(jnp.float32)
    info_all[row, pl.ds(pl.multiple_of(col * 8, 8), 8)] = info_ref[...]
    turned = rhs_ref[...].T
    res_ref[...] = turned
    direction = turned * (1.0 / cheb_center)
    dir_ref[...] = direction
    sol_ref[...] = direction
    dbf_ref[...] = direction.astype(jnp.bfloat16)
    for s in range(4):
        @pl.when(jnp.logical_not(has[s]))
        def _():
            for it in range(ITERS):
                for ref in recv_refs:
                    ref[it, s] = jnp.zeros(ref.shape[2:], jnp.float32)

    pl.semaphore_wait(barrier, n_gy - 1 + n_gx - 1)

    def gather_start(buf, height, g):
        mine = buf.at[row, pl.ds(pl.multiple_of(col * height, 8), height)]
        copies = []
        for k in range(1, n_gy):
            c = remote(mine, mine, gat_send.at[g, k], gat_recv.at[g, k], gy_peers[k - 1])
            c.start()
            copies.append(c)
        pending.extend(copies)
        return copies

    def gather_across(buf, g, copies):
        for c in copies:
            c.wait_recv()
        base = n_gy
        slab = buf.at[row]
        across = []
        for j in range(1, n_y):
            peer = (lax.rem(chip + j, n_y) * 2 + core, col)
            c = remote(slab, slab, gat_send.at[g, base + j], gat_recv.at[g, base + j], peer)
            c.start()
            across.append(c)
        base = n_gy + n_y
        c = remote(slab, slab, gat_send.at[g, base], gat_recv.at[g, base], sibling)
        c.start()
        pending.extend(across + [c])
        return across, [c]

    def gather_twin(buf, g, state):
        across, twin = state
        base = n_gy + n_y
        for j in range(1, n_y):
            across[j - 1].wait_recv()
            arrived = buf.at[lax.rem(chip + n_y - j, n_y) * 2 + core]
            c = remote(arrived, arrived, gat_send.at[g, base + j], gat_recv.at[g, base + j], sibling)
            c.start()
            twin.append(c)
        pending.extend(twin[1:])
        return twin

    def gather_end(twin):
        for c in twin:
            c.wait_recv()

    def side_copy(it, h, s):
        return remote(
            flexed_refs[h].at[it, s], recv_refs[h].at[it, OPP[s]],
            side_send.at[it, h, s], side_recv.at[it, h, OPP[s]], neighbour[s],
        )

    def side_arrival(it, h, s):
        return remote(
            flexed_refs[h].at[it, s], recv_refs[h].at[it, s],
            side_send.at[it, h, s], side_recv.at[it, h, s], neighbour[s],
        )

    def flex_product(h, s, inner):
        return folded(
            jnp.dot(
                flex_ref[s * side : (s + 1) * side, inner], dbf_ref[inner, lanes[h]],
                preferred_element_type=jnp.float32,
            ),
            h,
        )

    def send_side(it, h, s):
        @pl.when(has[s])
        def _():
            side_copy(it, h, s).start()

    info_g = 2 * ITERS
    info_copies = gather_start(info_all, 8, info_g)

    for s in range(4):
        flexed_refs[0][0, s] = flex_product(0, s, slice(0, order))
        send_side(0, 0, s)

    copy_cinv.wait()
    if cbf_ref.shape[1] > cols_c:
        cbf_ref[...] = jnp.zeros(cbf_ref.shape, jnp.bfloat16)
    cbf_ref[:, 0:cols_c] = cinv_ref[...].astype(jnp.bfloat16)
    info_state = gather_across(info_all, info_g, info_copies)
    for s in range(4):
        flexed_refs[1][0, s] = flex_product(1, s, slice(0, order))
        send_side(0, 1, s)
    gather_end(gather_twin(info_all, info_g, info_state))

    lane = lax.broadcasted_iota(jnp.int32, (corners, 128), 1)
    sub = lax.broadcasted_iota(jnp.int32, (corners, 128), 0)
    for a in range(n_gx):
        for b in range(n_gy):
            line = jnp.broadcast_to(info_all[a, b * 8 : b * 8 + 1, :], (corners, 128))
            column = jnp.sum(jnp.where(lane == sub, line, 0.0), axis=1, keepdims=True)
            ids_ref[a, b * corners : (b + 1) * corners, :] = jnp.broadcast_to(column, (corners, 128))

    strip = n_gy * corners
    row_iota = lax.broadcasted_iota(jnp.int32, (strip, rows_c), 1).astype(jnp.float32)
    to_core = []
    row_base = (row * rows_c).astype(jnp.float32)
    for a in range(n_gx):
        pick = jnp.where(ids_ref[a][:, 0:1] - row_base == row_iota, 1.0, 0.0).astype(jnp.bfloat16)
        part_ref[a] = jnp.dot(pick, cbf_ref[...], preferred_element_type=jnp.float32)
        if a % 2 == 1:
            j = a // 2
            c = remote(
                part_ref.at[2 * j + 1 - core], from_core.at[j], set_send.at[j], set_recv.at[j], sibling
            )
            c.start()
            to_core.append(c)
    pending.extend(to_core)

    def lines_at(a, b, entry):
        base = pl.multiple_of(b * 8, 8)
        return info_all[a, pl.ds(base, 8), :][1:2, entry : entry + 1]

    west_of = lax.rem(col + n_gy - 1, n_gy)
    north_of = lax.rem(row + n_gx - 1, n_gx)
    limits = (
        lines_at(row, west_of, 0) * jnp.where(has[0], 1.0, 0.0),
        lines_at(row, col, 0) * jnp.where(has[1], 1.0, 0.0),
        lines_at(north_of, col, 1) * jnp.where(has[2], 1.0, 0.0),
        lines_at(row, col, 1) * jnp.where(has[3], 1.0, 0.0),
    )

    def side_rows_of(h):
        shape = recv_refs[h].shape[2:]
        index = lax.broadcasted_iota(jnp.int32, shape, 0)
        at = lax.broadcasted_iota(jnp.int32, shape, 1)
        for i in range(1, folds[h]):
            index = index + jnp.where(at >= i * (loads - split), side // folds[h], 0)
        return index.astype(jnp.float32)

    side_iota = (side_rows_of(0), side_rows_of(1))

    for c in to_core:
        c.wait_recv()
    chunks = 2
    per_chunk = n_gy // chunks
    span = per_chunk * corners
    to_y = [[] for _ in range(chunks)]
    for j in range(1, n_y):
        target = lax.rem(chip + j, n_y)
        from_core[target] = from_core[target] + part_ref[2 * target + core]
        for q in range(chunks):
            rows_q = pl.ds(q * span, span)
            at = n_y + (j - 1) * chunks + q
            c = remote(
                from_core.at[target, rows_q], from_y.at[j - 1, rows_q], set_send.at[at], set_recv.at[at],
                (target * 2 + core, col),
            )
            c.start()
            to_y[q].append(c)
    for q in range(chunks):
        pending.extend(to_y[q])

    coarse = n_gy * cols_c
    col_iota = lax.broadcasted_iota(jnp.int32, (strip, coarse), 1).astype(jnp.float32)
    for a in range(n_gx):
        sel_ref[a * strip : (a + 1) * strip, :] = jnp.where(ids_ref[a][:, 0:1] == col_iota, 1.0, 0.0).astype(
            jnp.bfloat16
        )
    gy_base = n_y + (n_y - 1) * chunks

    def own_copy(b):
        return remote(
            own_rows.at[b], from_gy.at[col], set_send.at[gy_base + b], set_recv.at[gy_base + col], (row, b)
        )

    def own_arrival(b):
        return remote(
            own_rows.at[b], from_gy.at[b], set_send.at[gy_base + b], set_recv.at[gy_base + b], (row, b)
        )

    def set_spread(q):
        rows_q = slice(q * span, (q + 1) * span)
        own_strip = from_core[chip, rows_q] + part_ref[2 * chip + core, rows_q]
        for j in range(1, n_y):
            to_y[q][j - 1].wait_recv()
            own_strip = own_strip + from_y[j - 1, rows_q]
        for i in range(per_chunk):
            b = q * per_chunk + i
            own_rows[b] = own_strip[i * corners : (i + 1) * corners]

            @pl.when(b != col)
            def _():
                own_copy(b).start()

            @pl.when(b == col)
            def _():
                from_gy[b] = own_rows[b]

    def set_finish():
        for b in range(n_gy):
            @pl.when(b != col)
            def _():
                own_arrival(b).wait_recv()

        held = jnp.concatenate([from_gy[b][:, 0:cols_c] for b in range(n_gy)], axis=1).astype(jnp.bfloat16)
        coarse_ref[...] = lax.dot_general(
            held, sel_ref[...], (((1,), (1,)), ((), ())), preferred_element_type=jnp.float32
        )

    copy_stiff.wait()

    rho_prev = 1.0 / cheb_sigma
    for it in range(ITERS):
        last = it + 1 == ITERS
        if not last:
            rho_next = 1.0 / (2.0 * cheb_sigma - rho_prev)
            keep, gain = rho_next * rho_prev, 2.0 * rho_next / cheb_half
            rho_prev = rho_next

        def balance(h):
            for s in (2, 3, 0, 1):
                @pl.when(has[s])
                def _():
                    side_arrival(it, h, s).wait_recv()

                own = flexed_refs[h][it, s]
                jump = jnp.where(side_iota[h] < limits[s], recv_refs[h][it, s] - own, 0.0)
                bal_ref[s * side : (s + 1) * side, lanes[h]] = unfolded(own + 0.5 * jump, h).astype(jnp.bfloat16)

        def head_part(h):
            head = jnp.dot(stiff_ref[0:32, :], bal_ref[:, lanes[h]], preferred_element_type=jnp.float32)
            vals_refs[h][it, row, pl.ds(pl.multiple_of(col * corners, 8), corners)] = head[0:corners]
            return head, gather_start(vals_refs[h].at[it], corners, 2 * it + h)

        def rest_part(h, head):
            at = lanes[h]
            rest = jnp.dot(stiff_ref[32:, :], bal_ref[:, at], preferred_element_type=jnp.float32)
            mid = res_ref[corners:32, at] - head[corners:]
            low = res_ref[32:, at] - rest
            res_ref[corners:32, at] = mid
            res_ref[32:, at] = low
            squares = jnp.sum(low * low, axis=0, keepdims=True) + jnp.sum(mid * mid, axis=0, keepdims=True)
            if not last:
                later = keep * dir_ref[corners:, at] + gain * res_ref[corners:, at]
                dir_ref[corners:, at] = later
                sol_ref[corners:, at] = sol_ref[corners:, at] + later
                dbf_ref[128:, at] = later[128 - corners :].astype(jnp.bfloat16)
            return squares

        def flex_main(h):
            if not last:
                whole = jnp.dot(
                    flex_ref[:, 128:], dbf_ref[128:, lanes[h]], preferred_element_type=jnp.float32
                )
                for s in range(4):
                    flexed_refs[h][it + 1, s] = folded(whole[s * side : (s + 1) * side], h)

        def correct(h, head, squares):
            at = lanes[h]
            fixed = head[0:corners] + jnp.dot(
                coarse_ref[...].astype(jnp.bfloat16),
                vals_refs[h][it].reshape(n_sub * corners, vals_refs[h].shape[3]).astype(jnp.bfloat16),
                preferred_element_type=jnp.float32,
            )
            top = res_ref[0:corners, at] - fixed
            res_ref[0:corners, at] = top
            norm_gy[col, it : it + 1, at] = squares + jnp.sum(top * top, axis=0, keepdims=True)
            if not last:
                later = keep * dir_ref[0:corners, at] + gain * top
                dir_ref[0:corners, at] = later
                sol_ref[0:corners, at] = sol_ref[0:corners, at] + later
                dbf_ref[0:128, at] = dir_ref[0:128, at].astype(jnp.bfloat16)
                for s in range(4):
                    flexed_refs[h][it + 1, s] += flex_product(h, s, slice(0, 128))
                    send_side(it + 1, h, s)

        bufs = (vals_0.at[it], vals_1.at[it])
        balance(0)
        head_0, copies_0 = head_part(0)
        squares_0 = rest_part(0, head_0)
        if it == 0:
            for q in range(chunks):
                set_spread(q)
        balance(1)
        head_1, copies_1 = head_part(1)
        state_0 = gather_across(bufs[0], 2 * it, copies_0)
        flex_main(0)
        twin_0 = gather_twin(bufs[0], 2 * it, state_0)
        squares_1 = rest_part(1, head_1)
        state_1 = gather_across(bufs[1], 2 * it + 1, copies_1)
        if it == 0:
            set_finish()
        gather_end(twin_0)
        correct(0, head_0, squares_0)
        flex_main(1)
        twin_1 = gather_twin(bufs[1], 2 * it + 1, state_1)
        gather_end(twin_1)
        correct(1, head_1, squares_1)

    mine = norm_gy.at[col]
    sums = []
    for k in range(1, n_gy):
        c = remote(mine, mine, nrm_send.at[k], nrm_recv.at[k], gy_peers[k - 1])
        c.start()
        sums.append(c)
    for c in sums:
        c.wait_recv()
    total = norm_gy[0, 0:ITERS]
    for b in range(1, n_gy):
        total = total + norm_gy[b, 0:ITERS]
    norm_gx[row, 0:ITERS] = total
    mine = norm_gx.at[row]
    wide = []
    for k in range(1, n_gx):
        c = remote(mine, mine, nrm_send.at[n_gy + k], nrm_recv.at[n_gy + k], gx_peers[k - 1])
        c.start()
        wide.append(c)
    for c in wide:
        c.wait_recv()
    total = norm_gx[0, 0:ITERS]
    for a in range(1, n_gx):
        total = total + norm_gx[a, 0:ITERS]
    norm_ref[...] = jnp.sqrt(total / (n_sub * order))

    for c in pending + sums + wide:
        c.wait_send()
    for b in range(n_gy):
        @pl.when(b != col)
        def _():
            own_copy(b).wait_send()

    for s in range(4):
        @pl.when(has[s])
        def _():
            for it in range(ITERS):
                for h in range(2):
                    side_copy(it, h, s).wait_send()


def local(right_side, flex, stiff, coarse_inv, corner_map, side_rows):
    n_gx = lax.axis_size("gx")
    n_gy = lax.axis_size("gy")
    n_y = n_gx // 2
    loads, order = right_side.shape[2:]
    corners = corner_map.shape[2]
    side = order // 4
    rows_c, cols_c = coarse_inv.shape
    strip = n_gy * corners
    split = 128
    width = loads - split
    fold = 2 if 2 * width <= 128 else 1
    cols_p = -(-cols_c // 128) * 128
    f32, bf16 = jnp.float32, jnp.bfloat16
    vmem = pl.BlockSpec(memory_space=pltpu.VMEM)
    hbm = pl.BlockSpec(memory_space=pl.ANY)
    n_gather = n_gy + 2 * n_y
    n_setup = 3 * n_y + n_gy
    dma = pltpu.SemaphoreType.DMA
    sol, res, norm = pl.pallas_call(
        functools.partial(kernel, n_gx, n_gy, corners, split, fold),
        out_shape=(
            jax.ShapeDtypeStruct((order, loads), f32),
            jax.ShapeDtypeStruct((order, loads), f32),
            jax.ShapeDtypeStruct((ITERS, loads), f32),
        ),
        in_specs=[vmem, vmem, hbm, hbm, vmem, vmem],
        out_specs=(vmem, vmem, vmem),
        scratch_shapes=[
            pltpu.VMEM((order, order), bf16),
            pltpu.VMEM((rows_c, cols_c), f32),
            pltpu.VMEM((rows_c, cols_p), bf16),
            pltpu.VMEM((8, 128), f32),
            pltpu.VMEM((n_gx, n_gy * 8, 128), f32),
            pltpu.VMEM((n_gx, strip, 128), f32),
            pltpu.VMEM((n_gx, strip, cols_p), f32),
            pltpu.VMEM((n_y, strip, cols_p), f32),
            pltpu.VMEM((n_y, strip, cols_p), f32),
            pltpu.VMEM((n_gy, corners, cols_p), f32),
            pltpu.VMEM((n_gy, corners, cols_p), f32),
            pltpu.VMEM((corners, n_gx * strip), f32),
            pltpu.VMEM((n_gx * strip, n_gy * cols_c), bf16),
            pltpu.VMEM((order, loads), f32),
            pltpu.VMEM((order, loads), bf16),
            pltpu.VMEM((order, loads), bf16),
            pltpu.VMEM((ITERS, 4, side, split), f32),
            pltpu.VMEM((ITERS, 4, side // fold, width * fold), f32),
            pltpu.VMEM((ITERS, 4, side, split), f32),
            pltpu.VMEM((ITERS, 4, side // fold, width * fold), f32),
            pltpu.VMEM((ITERS, n_gx, strip, split), f32),
            pltpu.VMEM((ITERS, n_gx, strip, width), f32),
            pltpu.VMEM((n_gy, 8, loads), f32),
            pltpu.VMEM((n_gx, 8, loads), f32),
            dma((2,)),
            dma((ITERS, 2, 4)),
            dma((ITERS, 2, 4)),
            dma((2 * ITERS + 1, n_gather)),
            dma((2 * ITERS + 1, n_gather)),
            dma((n_setup,)),
            dma((n_setup,)),
            dma((n_gy + n_gx,)),
            dma((n_gy + n_gx,)),
        ],
        compiler_params=pltpu.CompilerParams(
            collective_id=0, has_side_effects=True, vmem_limit_bytes=57 * 1024 * 1024
        ),
    )(right_side[0, 0], flex[0, 0], stiff[0, 0], coarse_inv, corner_map[0], side_rows[0])
    return (sol.T[None, None], res.T[None, None], norm)


def solution(mesh):
    placed = (
        P("gx", "gy", None, None),
        P("gx", "gy", None, None),
        P("gx", "gy", None, None),
        P("gx", "gy"),
        P("gx", "gy", None),
        P("gx", "gy", None),
    )
    return jax.shard_map(
        local,
        mesh=mesh,
        in_specs=placed,
        out_specs=(P("gx", "gy", None, None), P("gx", "gy", None, None), P()),
        check_vma=False,
    )
```
